512 devices in a mesh: node: 8 (over z_hi, core), dp: 64 (over y, x, z_lo).
Axes of the slice: x: 4, y: 4, z: 16 (z_hi: 4, z_lo: 4; z = z_hi * 4 + z_lo), core: 2. Of those that a mesh axis runs over, the one named last changes fastest.
Arguments:
- inputs: bfloat16 [393216, 896], P(('node', 'dp')), may hold values from -24 to 24
- cotangent: bfloat16 [393216, 1152], P(('node', 'dp')), may hold values from -6 to 6
- weight: bfloat16 [896, 1152], P('node'), may hold values from -0.1875 to 0.1875
- moment_one: float32 [1032192], P(('node', 'dp')), may hold values from -0.0068359375 to 0.0068359375
- moment_two: float32 [1032192], P(('node', 'dp')), may hold values from 2.5431316e-07 to 2.5431316e-06
Outputs:
- grad_in: bfloat16 [393216, 896], P(('node', 'dp'))
- update: float32 [1032192], P(('node', 'dp'))
- new_weight: bfloat16 [896, 1152], P('node')
The draws below stay inside these ranges and needn't reach their ends.
All inputs are finite; a program needn't handle non-finite values.
Results may differ from the reference program's by a relative error of at most 0.007.
Values may be sent and summed in bfloat16 or wider, within the bound.
No kernel may reach another device: no remote copies, remote signals or barrier semaphores. Data moves between devices by JAX's collectives and lax.ppermute only.
A program may use at most 64 MiB of HBM per device.

```python
import math
import jax
import jax.numpy as jnp
from jax import lax

D = 896
TOK_DEV = 768
STEP = 10
QKV = 1152
TOKENS = 393216
N_NODE = 8
N_DP = 64


def with_spikes(array, rng, source, target, blocks, factor):
    def block_of(axis_at):
        return (jnp.arange(array.shape[axis_at]) // (array.shape[axis_at] // blocks)).reshape((-1,) + (1,) * (array.ndim - 1 - axis_at))

    one_side = jax.random.permutation(rng, blocks)[block_of(target)]
    far = (block_of(target) + blocks // 2) % blocks
    return jnp.where((block_of(source) == one_side) | (block_of(source) == far), factor * array, array)


def block_scale(rng, extent, shards, low, high):
    def one(position, shards_of):
        heights = jax.random.uniform(jax.random.fold_in(jax.random.fold_in(rng, 6), position), (shards_of,), jnp.float32, low / len(shards), high / len(shards))
        return jnp.repeat(jnp.exp(heights), extent[position] // shards_of).reshape((-1,) + (1,) * (len(extent) - position - 1))

    factor_of = one(*shards[0])
    for cut in shards[1:]:
        factor_of = factor_of * one(*cut)
    return factor_of


def bell_draw(own_key, dims, deviation, bound, split=(), kind=jnp.bfloat16):
    level = block_scale(own_key, dims, split, -0.22, 0.18) if split else 1.0
    array = jax.random.normal(own_key, dims, jnp.float32) * deviation * level
    return jnp.minimum(jnp.maximum(array, -bound), bound).astype(kind)


def bell_draw_with(own_key, extent, deviation, bound, split, heavy, kind=jnp.bfloat16):
    drawn = deviation * jax.random.normal(own_key, extent, jnp.float32)
    if split:
        drawn = drawn * block_scale(own_key, extent, split, -0.22, 0.18)
    return jnp.clip(with_spikes(drawn, jax.random.fold_in(own_key, 3), *heavy), -bound, bound).astype(kind)


def setup_inputs(seed: int = 0) -> dict:
    key_list = jax.random.split(jax.random.key(seed), 6)
    return {
        "inputs": bell_draw_with(key_list[0], (TOKENS, D), 1.0, 24.0, ((0, 512),), (0, 1, 128, 5.5)),
        "cotangent": bell_draw(key_list[1], (TOKENS, QKV), 1.0, 6.0, ((0, 512),)),
        "weight": bell_draw(key_list[2], (D, QKV), D ** -0.5, 0.1875, ((0, 8),)),
        "moment_one": bell_draw(key_list[3], (D * QKV,), (0.3 * TOKENS ** -0.5), 0.0068359375, ((0, 512),), jnp.float32),
        "moment_two": jnp.clip(jnp.exp(math.log(2.543131586207892e-06) - 2.3025851 * jax.random.uniform(key_list[4], (D * QKV,), jnp.float32) ** block_scale(key_list[4], (D * QKV,), ((0, 512),), -0.2, 0.2)), 2.5431316430513107e-07, 2.543131586207892e-06),
    }


def reference(inputs, cotangent, weight, moment_one, moment_two):
    grad_in = jnp.dot(cotangent, weight.T, preferred_element_type=jnp.float32).astype(jnp.bfloat16)
    devices_all = N_NODE * N_DP
    input_blocks = inputs.reshape(devices_all, TOK_DEV, D)
    cot_blocks = cotangent.reshape(devices_all, TOK_DEV, QKV)

    def add_block(total, pair):
        block_in, block_cot = pair
        partial_term = jnp.dot(block_in.T, block_cot, preferred_element_type=jnp.float32).astype(jnp.bfloat16)
        partial_term = lax.optimization_barrier(partial_term)
        return (total + partial_term.astype(jnp.float32), None)
    summed, _ = lax.scan(add_block, jnp.zeros((D, QKV), jnp.float32), (input_blocks, cot_blocks))
    gradient = (summed * (1.0 / TOKENS)).reshape(-1)
    first = 0.9 * moment_one + 0.1 * gradient
    second = 0.95 * moment_two + 0.05 * gradient * gradient
    update = first / (1.0 - 0.9 ** STEP) / (jnp.sqrt(second / (1.0 - 0.95 ** STEP)) + 1e-08)
    current = weight.reshape(-1).astype(jnp.float32)
    stepped = (current - 0.005 * (update + 0.1 * current)).astype(jnp.bfloat16)
    return (grad_in, update, stepped.reshape(D, QKV))
```

```python
import jax
import jax.numpy as jnp
import numpy as np
from jax import lax
from jax.sharding import Mesh, PartitionSpec as P

STEP = 10
AXES = ("zh", "core", "y", "x", "zl")
SIZES = (4, 2, 4, 4, 4)


def selection():
    pick = np.zeros((2, 16, 4, 8, 896), np.float32)
    for core in range(2):
        for yx in range(16):
            for zh in range(4):
                for r in range(7):
                    pick[core, yx, zh, r, zh * 224 + core * 112 + yx * 7 + r] = 1.0
    return pick.reshape(1024, 896)


def shards(inputs, cotangent, weight, moment_one, moment_two):
    bf16, f32 = jnp.bfloat16, jnp.float32
    core = lax.axis_index("core")
    turned = jnp.einsum(
        "pr,tr->pt", jnp.asarray(selection(), bf16), inputs, preferred_element_type=f32
    ).astype(bf16).reshape(2, 512, 768)
    theirs = lax.dynamic_index_in_dim(turned, 1 - core, 0, keepdims=False)
    mine = lax.dynamic_index_in_dim(turned, core, 0, keepdims=False)
    send = jnp.dot(theirs, cotangent, preferred_element_type=f32).astype(bf16)
    got = lax.ppermute(send, "core", [(0, 1), (1, 0)])
    kept = jnp.dot(mine, cotangent, preferred_element_type=f32).astype(bf16)
    chip = (kept.astype(f32) + got.astype(f32)).astype(bf16).reshape(16, 4, 8, 1152)
    plane = lax.all_to_all(chip, ("y", "x"), 0, 0)
    plane = jnp.sum(plane.astype(f32), axis=0)
    quarters = plane[:, :7].astype(bf16).reshape(16, 1, 2016)
    column = lax.all_to_all(quarters, ("zh", "zl"), 0, 0)
    gradient = jnp.sum(column.astype(f32), axis=0).reshape(2016) * (1.0 / 393216)

    own = (lax.axis_index("y") * 4 + lax.axis_index("x")) * 4 + lax.axis_index("zl")
    current = lax.dynamic_slice_in_dim(weight.reshape(-1), own * 2016, 2016, 0).astype(f32)
    first = 0.9 * moment_one + 0.1 * gradient
    second = 0.95 * moment_two + 0.05 * gradient * gradient
    update = first / (1.0 - 0.9**STEP) / (jnp.sqrt(second / (1.0 - 0.95**STEP)) + 1e-08)
    stepped = (current - 0.005 * (update + 0.1 * current)).astype(bf16)
    spread = jnp.broadcast_to(stepped.reshape(1, 1, 2016), (64, 1, 2016))
    new_weight = lax.all_to_all(spread, ("y", "x", "zl"), 0, 0).reshape(112, 1152)

    whole = lax.all_gather(weight, ("zh", "core"), axis=0, tiled=True)
    grad_in = jnp.einsum("tq,rq->tr", cotangent, whole, preferred_element_type=f32).astype(bf16)
    return (grad_in, update, new_weight)


def solution(mesh):
    fine = Mesh(mesh.devices.reshape(SIZES), AXES)
    return jax.shard_map(
        shards,
        mesh=fine,
        in_specs=(
            P(AXES, None),
            P(AXES, None),
            P(("zh", "core"), None),
            P(AXES),
            P(AXES),
        ),
        out_specs=(P(AXES, None), P(AXES), P(("zh", "core"), None)),
        check_vma=False,
    )
```

```python
import jax
import jax.numpy as jnp
from jax import lax
from jax.experimental import pallas as pl
from jax.experimental.pallas import tpu as pltpu
from jax.sharding import Mesh, PartitionSpec as P

STEP = 10
AXES = ("zh", "core", "y", "x", "zl")
SIZES = (4, 2, 4, 4, 4)
BF16, F32 = jnp.bfloat16, jnp.float32
VMEM = pl.BlockSpec(memory_space=pltpu.VMEM)
SMEM = pl.BlockSpec(memory_space=pltpu.SMEM)
PARAMS = pltpu.CompilerParams(vmem_limit_bytes=40 * 1024 * 1024)


def term_kernel(half_ref, x_ref, c_ref, out_ref):
    half = half_ref[0]
    for pair in range(2):
        low = 384 * pair
        place = lax.broadcasted_iota(jnp.int32, (256, 512), 0)
        column = lax.broadcasted_iota(jnp.int32, (256, 512), 1)
        row = place & 7
        source = (2 * pair + ((place >> 3) & 1)) * 224 + half * 112 + (place >> 4) * 7 + row - low
        pick = jnp.where((source == column) & (row < 7), 1.0, 0.0).astype(BF16)
        turned = lax.dot_general(
            pick, x_ref[:, low : low + 512], (((1,), (1,)), ((), ())), preferred_element_type=F32
        ).astype(BF16)
        part = jnp.dot(turned, c_ref[...], preferred_element_type=F32).astype(BF16)
        out_ref[:, 16 * pair : 16 * pair + 16, :] = part.reshape(16, 16, 1152)


def quarters_kernel(plane_ref, tile_ref, out_ref, flat_ref):
    total = plane_ref[0].astype(F32)
    for i in range(1, 16):
        total = total + plane_ref[i].astype(F32)
    lane = lax.broadcasted_iota(jnp.int32, (16, 128), 1)
    tile = tile_ref[...]
    for zh in range(4):
        for k in range(9):
            flat_ref[zh, pl.ds(k, 8, stride=9), :] = total[8 * zh : 8 * zh + 8, 128 * k : 128 * k + 128]
        for q in range(4):
            row, off = divmod(2016 * q, 128)
            here = flat_ref[zh, row : row + 16, :]
            if off:
                after = flat_ref[zh, row + 1 : row + 17, :]
                here = jnp.where(
                    lane < 128 - off,
                    pltpu.roll(here, 128 - off, axis=1),
                    pltpu.roll(after, 128 - off, axis=1),
                )
            out_ref[4 * zh + q, 0:16, :] = here.astype(BF16)
            out_ref[4 * zh + q, 16:32, :] = tile


def step_kernel(column_ref, one_ref, two_ref, current_ref, update_ref, tiles_ref, stepped_ref):
    gradient = column_ref[0, 0:16, :].astype(F32)
    for i in range(1, 16):
        gradient = gradient + column_ref[i, 0:16, :].astype(F32)
    gradient = gradient * (1.0 / 393216)
    current = current_ref[...]
    first = 0.9 * one_ref[...] + 0.1 * gradient
    second = 0.95 * two_ref[...] + 0.05 * gradient * gradient
    update = first / (1.0 - 0.9**STEP) / (jnp.sqrt(second / (1.0 - 0.95**STEP)) + 1e-08)
    update_ref[...] = update
    stepped = (current - 0.005 * (update + 0.1 * current)).astype(BF16)
    for i in range(64):
        stepped_ref[i] = stepped
    for z in range(16):
        tile = column_ref[z, 16:32, :]
        for i in range(16):
            tiles_ref[i, z] = tile


def rows_kernel(piece_ref, out_ref, flat_ref, rows_ref):
    lane = lax.broadcasted_iota(jnp.int32, (16, 128), 1)
    line = lax.broadcasted_iota(jnp.int32, (16, 128), 0)
    for p in range(16):
        for q in range(4):
            row, off = divmod(2016 * q, 128)
            piece = piece_ref[4 * p + q].astype(F32)
            if off:
                piece = pltpu.roll(piece, off, axis=1)
                above = pltpu.roll(piece, 1, axis=0)
                old = flat_ref[p, row : row + 16, :]
                flat_ref[p, row + 16 : row + 17, :] = piece[15:16, :]
                piece = jnp.where(lane >= off, piece, jnp.where(line == 0, old, above))
            flat_ref[p, row : row + 16, :] = piece
        for k in range(9):
            rows_ref[7 * p : 7 * p + 7, 128 * k : 128 * k + 128] = flat_ref[p, pl.ds(k, 7, stride=9), :]
    out_ref[...] = rows_ref[...].astype(BF16)


def input_kernel(core_ref, c_ref, own_ref, other_ref, out_ref, whole_ref):
    core = core_ref[0]
    for ref, half in ((own_ref, core), (other_ref, 1 - core)):
        for zh in range(4):
            for t in range(63):
                low = pl.multiple_of(224 * zh + 112 * half + 16 * (t // 9), 16)
                whole_ref[pl.ds(low, 16), 128 * (t % 9) : 128 * (t % 9) + 128] = ref[t // 4, 4 * zh + t % 4]
    out_ref[...] = lax.dot_general(
        c_ref[...], whole_ref[...], (((1,), (1,)), ((), ())), preferred_element_type=F32
    ).astype(BF16)


def call(kernel, outs, operands, specs, scratch=()):
    return pl.pallas_call(
        kernel,
        out_shape=outs,
        in_specs=specs,
        out_specs=jax.tree.map(lambda _: VMEM, outs),
        scratch_shapes=list(scratch),
        compiler_params=PARAMS,
    )(*operands)


def shards(inputs, cotangent, weight, moment_one, moment_two):
    shape = jax.ShapeDtypeStruct
    core = lax.axis_index("core").astype(jnp.int32).reshape(1)
    own = (lax.axis_index("y") * 4 + lax.axis_index("x")) * 4 + lax.axis_index("zl")

    def term(half):
        return call(term_kernel, shape((16, 32, 1152), BF16), (half, inputs, cotangent), [SMEM, VMEM, VMEM])

    send = term(1 - core)
    got = lax.ppermute(send, "core", [(0, 1), (1, 0)])
    kept = term(core)
    chip = (kept.astype(F32) + got.astype(F32)).astype(BF16)
    plane = lax.all_to_all(chip, ("y", "x"), 0, 0)

    own_tile = jnp.minimum(own, 62)
    tile = lax.dynamic_slice(weight, (16 * (own_tile // 9), 128 * (own_tile % 9)), (16, 128))
    current = lax.dynamic_slice_in_dim(weight.reshape(-1), own * 2016, 2016, 0)
    padded = [jnp.pad(a.astype(F32), (0, 32)).reshape(16, 128) for a in (moment_one, moment_two, current)]
    quarters = call(
        quarters_kernel,
        shape((16, 32, 128), BF16),
        (plane, tile),
        [VMEM, VMEM],
        [pltpu.VMEM((4, 72, 128), F32)],
    )
    column = lax.all_to_all(quarters, ("zh", "zl"), 0, 0)
    update, tiles, stepped = call(
        step_kernel,
        (shape((16, 128), F32), shape((16, 16, 16, 128), BF16), shape((64, 16, 128), BF16)),
        (column, *padded),
        [VMEM] * 4,
    )
    tiles = lax.all_to_all(tiles, ("y", "x"), 0, 0)
    stepped = lax.all_to_all(stepped, ("y", "x", "zl"), 0, 0)
    others = lax.ppermute(tiles, "core", [(0, 1), (1, 0)])
    new_weight = call(
        rows_kernel,
        shape((112, 1152), BF16),
        (stepped,),
        [VMEM],
        [pltpu.VMEM((16, 72, 128), F32), pltpu.VMEM((112, 1152), F32)],
    )
    grad_in = call(
        input_kernel,
        shape((768, 896), BF16),
        (core, cotangent, tiles, others),
        [SMEM, VMEM, VMEM, VMEM],
        [pltpu.VMEM((896, 1152), BF16)],
    )
    return (grad_in, update.reshape(2048)[:2016], new_weight)


def solution(mesh):
    fine = Mesh(mesh.devices.reshape(SIZES), AXES)
    return jax.shard_map(
        shards,
        mesh=fine,
        in_specs=(
            P(AXES, None),
            P(AXES, None),
            P(("zh", "core"), None),
            P(AXES),
            P(AXES),
        ),
        out_specs=(P(AXES, None), P(AXES), P(("zh", "core"), None)),
        check_vma=False,
    )
```

```python
import jax
import jax.numpy as jnp
from jax import lax
from jax.experimental import pallas as pl
from jax.experimental.pallas import tpu as pltpu
from jax.sharding import Mesh, PartitionSpec as P

STEP = 10
AXES = ("zh", "core", "y", "x", "zl")
SIZES = (4, 2, 4, 4, 4)
BF16, F32 = jnp.bfloat16, jnp.float32
VMEM = pl.BlockSpec(memory_space=pltpu.VMEM)
SMEM = pl.BlockSpec(memory_space=pltpu.SMEM)
PARAMS = pltpu.CompilerParams(vmem_limit_bytes=16 * 1024 * 1024)


def term_kernel(half_ref, x_ref, c_ref, out_ref):
    half = half_ref[0]
    for pair in range(2):
        low = 384 * pair
        place = lax.broadcasted_iota(jnp.int32, (256, 512), 0)
        column = lax.broadcasted_iota(jnp.int32, (256, 512), 1)
        row = place & 7
        source = (2 * pair + ((place >> 3) & 1)) * 224 + half * 112 + (place >> 4) * 7 + row - low
        pick = jnp.where((source == column) & (row < 7), 1.0, 0.0).astype(BF16)
        turned = lax.dot_general(
            pick, x_ref[:, low : low + 512], (((1,), (1,)), ((), ())), preferred_element_type=F32
        ).astype(BF16)
        part = jnp.dot(turned, c_ref[...], preferred_element_type=F32).astype(BF16)
        out_ref[:, 16 * pair : 16 * pair + 16, :] = part.reshape(16, 16, 1152)


def column_kernel(plane_ref, tile_ref, out_ref, flat_ref):
    total = plane_ref[0].astype(F32)
    for i in range(1, 16):
        total = total + plane_ref[i].astype(F32)
    tile = tile_ref[...]
    for zh in range(4):
        for k in range(9):
            flat_ref[zh, pl.ds(k, 8, stride=9), :] = total[8 * zh : 8 * zh + 8, 128 * k : 128 * k + 128]
        flat = flat_ref[zh, 0:64, :].astype(BF16)
        for zl in range(4):
            out_ref[4 * zh + zl, 0:64, :] = flat
            out_ref[4 * zh + zl, 64:80, :] = tile


def lay(flat_ref, pieces):
    lane = lax.broadcasted_iota(jnp.int32, (16, 128), 1)
    line = lax.broadcasted_iota(jnp.int32, (16, 128), 0)
    for q in range(4):
        row, off = divmod(2016 * q, 128)
        piece = pieces[q]
        if off:
            piece = pltpu.roll(piece, off, axis=1)
            above = pltpu.roll(piece, 1, axis=0)
            old = flat_ref[row : row + 16, :]
            flat_ref[row + 16 : row + 17, :] = piece[15:16, :]
            piece = jnp.where(lane >= off, piece, jnp.where(line == 0, old, above))
        flat_ref[row : row + 16, :] = piece
    return flat_ref[0:64, :]


def cut(flat_ref, q):
    lane = lax.broadcasted_iota(jnp.int32, (16, 128), 1)
    row, off = divmod(2016 * q, 128)
    here = flat_ref[row : row + 16, :]
    if off:
        after = flat_ref[row + 1 : row + 17, :]
        here = jnp.where(
            lane < 128 - off, pltpu.roll(here, 128 - off, axis=1), pltpu.roll(after, 128 - off, axis=1)
        )
    return here


def step_kernel(
    zl_ref, zh_ref, column_ref, own_ref, m1_ref, m2_ref, m3_ref, current_ref, update_ref, out_ref, quarter_ref, flat_ref
):
    zl = zl_ref[0]
    quarter_ref[zl] = own_ref[...]
    quarter_ref[zl ^ 1] = m1_ref[...]
    quarter_ref[zl ^ 2] = m2_ref[...]
    quarter_ref[zl ^ 3] = m3_ref[...]
    flat_ref[...] = jnp.zeros_like(flat_ref)
    one = lay(flat_ref.at[0], [quarter_ref[q, 0] for q in range(4)])
    two = lay(flat_ref.at[1], [quarter_ref[q, 1] for q in range(4)])
    for k in range(9):
        flat_ref[2, pl.ds(k, 8, stride=9), :] = current_ref[:, 128 * k : 128 * k + 128]
    current = flat_ref[2, 0:64, :]
    gradient = column_ref[0, 0:64, :].astype(F32)
    for i in range(1, 16):
        gradient = gradient + column_ref[i, 0:64, :].astype(F32)
    gradient = gradient * (1.0 / 393216)
    first = 0.9 * one + 0.1 * gradient
    second = 0.95 * two + 0.05 * gradient * gradient
    update = first / (1.0 - 0.9**STEP) / (jnp.sqrt(second / (1.0 - 0.95**STEP)) + 1e-08)
    stepped = (current - 0.005 * (update + 0.1 * current)).astype(BF16)
    for i in range(16):
        out_ref[i, 0:64, :] = stepped
    zh = zh_ref[0]
    for slot in range(12):
        tile = column_ref[4 * (zh ^ (slot // 4 + 1)) + slot % 4, 64:80, :]
        for i in range(16):
            out_ref[i, 64 + 16 * slot : 80 + 16 * slot, :] = tile
    flat_ref[3, 0:64, :] = update
    for q in range(4):
        quarter_ref[q, 0] = cut(flat_ref.at[3], q)
    update_ref[...] = quarter_ref[zl, 0]


def rows_kernel(piece_ref, out_ref, flat_ref, rows_ref):
    for p in range(16):
        flat_ref[p, 0:64, :] = piece_ref[p, 0:64, :].astype(F32)
        for k in range(9):
            rows_ref[7 * p : 7 * p + 7, 128 * k : 128 * k + 128] = flat_ref[p, pl.ds(k, 7, stride=9), :]
    out_ref[...] = rows_ref[...].astype(BF16)


def input_kernel(core_ref, zh_ref, c_ref, mine_ref, yours_ref, own_ref, other_ref, out_ref, whole_ref):
    core, zh = core_ref[0], zh_ref[0]
    for rows_ref, ref, half in ((mine_ref, own_ref, core), (yours_ref, other_ref, 1 - core)):
        whole_ref[pl.ds(pl.multiple_of(224 * zh + 112 * half, 16), 112), :] = rows_ref[...]
        for d in (1, 2, 3):
            for t in range(63):
                low = pl.multiple_of(224 * (zh ^ d) + 112 * half + 16 * (t // 9), 16)
                slot = 64 + 16 * (4 * (d - 1) + t % 4)
                whole_ref[pl.ds(low, 16), 128 * (t % 9) : 128 * (t % 9) + 128] = ref[t // 4, slot : slot + 16, :]
    out_ref[...] = lax.dot_general(
        c_ref[...], whole_ref[...], (((1,), (1,)), ((), ())), preferred_element_type=F32
    ).astype(BF16)


def call(kernel, outs, operands, specs, scratch=()):
    return pl.pallas_call(
        kernel,
        out_shape=outs,
        in_specs=specs,
        out_specs=jax.tree.map(lambda _: VMEM, outs),
        scratch_shapes=list(scratch),
        compiler_params=PARAMS,
    )(*operands)


def shards(inputs, cotangent, weight, moment_one, moment_two):
    shape = jax.ShapeDtypeStruct
    core = lax.axis_index("core").astype(jnp.int32).reshape(1)
    zl, zh = (lax.axis_index(a).astype(jnp.int32).reshape(1) for a in ("zl", "zh"))
    own = (lax.axis_index("y") * 4 + lax.axis_index("x")) * 4 + lax.axis_index("zl")

    def term(half):
        return call(term_kernel, shape((16, 32, 1152), BF16), (half, inputs, cotangent), [SMEM, VMEM, VMEM])

    send = term(1 - core)
    got = lax.ppermute(send, "core", [(0, 1), (1, 0)])
    kept = term(core)
    chip = (kept.astype(F32) + got.astype(F32)).astype(BF16)
    own_tile = jnp.minimum(own, 62)
    tile = lax.dynamic_slice(weight, (16 * (own_tile // 9), 128 * (own_tile % 9)), (16, 128))
    current = lax.dynamic_slice(weight, (7 * (own // 4), 0), (7, 1152))
    current = jnp.pad(current.astype(F32), ((0, 1), (0, 0)))
    moments = jnp.stack([jnp.pad(a, (0, 32)).reshape(16, 128) for a in (moment_one, moment_two)])
    moments, mine, chip = lax.optimization_barrier((moments, weight, chip))
    plane = lax.all_to_all(chip, ("y", "x"), 0, 0)
    near = [lax.ppermute(moments, "zl", [(i, i ^ d) for i in range(4)]) for d in (1, 2, 3)]
    yours = lax.ppermute(mine, "core", [(0, 1), (1, 0)])
    plane, yours, *near = lax.optimization_barrier((plane, yours, *near))
    column = call(
        column_kernel,
        shape((16, 80, 128), BF16),
        (plane, tile),
        [VMEM, VMEM],
        [pltpu.VMEM((4, 72, 128), F32)],
    )
    column = lax.all_to_all(column, ("zh", "zl"), 0, 0)
    update, spread = call(
        step_kernel,
        (shape((16, 128), F32), shape((16, 256, 128), BF16)),
        (zl, zh, column, moments, *near, current),
        [SMEM] * 2 + [VMEM] * 6,
        [pltpu.VMEM((4, 2, 16, 128), F32), pltpu.VMEM((4, 80, 128), F32)],
    )
    spread = lax.all_to_all(spread, ("y", "x"), 0, 0)
    others = lax.ppermute(spread, "core", [(0, 1), (1, 0)])
    new_weight = call(
        rows_kernel,
        shape((112, 1152), BF16),
        (spread,),
        [VMEM],
        [pltpu.VMEM((16, 72, 128), F32), pltpu.VMEM((112, 1152), F32)],
    )
    grad_in = call(
        input_kernel,
        shape((768, 896), BF16),
        (core, zh, cotangent, weight, yours, spread, others),
        [SMEM] * 2 + [VMEM] * 5,
        [pltpu.VMEM((896, 1152), BF16)],
    )
    return (grad_in, update.reshape(2048)[:2016], new_weight)


def solution(mesh):
    fine = Mesh(mesh.devices.reshape(SIZES), AXES)
    return jax.shard_map(
        shards,
        mesh=fine,
        in_specs=(
            P(AXES, None),
            P(AXES, None),
            P(("zh", "core"), None),
            P(AXES),
            P(AXES),
        ),
        out_specs=(P(AXES, None), P(AXES), P(("zh", "core"), None)),
        check_vma=False,
    )
```

```python
import jax
import jax.numpy as jnp
from jax import lax
from jax.experimental import pallas as pl
from jax.experimental.pallas import tpu as pltpu
from jax.sharding import Mesh, PartitionSpec as P

STEP = 10
AXES = ("zh", "core", "y", "x", "zb", "za")
SIZES = (4, 2, 4, 4, 2, 2)
BF16, F32 = jnp.bfloat16, jnp.float32
VMEM = pl.BlockSpec(memory_space=pltpu.VMEM)
SMEM = pl.BlockSpec(memory_space=pltpu.SMEM)
PARAMS = pltpu.CompilerParams(vmem_limit_bytes=16 * 1024 * 1024)


def turn_kernel(x_ref, out_ref):
    for half in range(2):
        for pair in range(2):
            low = 384 * pair
            place = lax.broadcasted_iota(jnp.int32, (256, 512), 0)
            column = lax.broadcasted_iota(jnp.int32, (256, 512), 1)
            row = place & 7
            source = (2 * pair + ((place >> 3) & 1)) * 224 + half * 112 + (place >> 4) * 7 + row - low
            pick = jnp.where((source == column) & (row < 7), 1.0, 0.0).astype(BF16)
            out_ref[half, pair] = lax.dot_general(
                pick, x_ref[:, low : low + 512], (((1,), (1,)), ((), ())), preferred_element_type=F32
            ).astype(BF16)


def term_kernel(half_ref, turned_ref, c_ref, out_ref):
    for pair in range(2):
        part = jnp.dot(turned_ref[half_ref[0], pair], c_ref[...], preferred_element_type=F32).astype(BF16)
        out_ref[:, 16 * pair : 16 * pair + 16, :] = part.reshape(16, 16, 1152)


def add_kernel(kept_ref, got_ref, out_ref):
    for p in range(16):
        out_ref[p] = kept_ref[p] + got_ref[p]


def column_kernel(plane_ref, tile_ref, out_ref, flat_ref):
    total = plane_ref[0].astype(F32)
    for i in range(1, 16):
        total = total + plane_ref[i].astype(F32)
    tile = tile_ref[...]
    for zh in range(4):
        for k in range(9):
            flat_ref[zh, pl.ds(k, 8, stride=9), :] = total[8 * zh : 8 * zh + 8, 128 * k : 128 * k + 128]
        quarters = [cut(flat_ref.at[zh], q).astype(BF16) for q in range(4)]
        for zl in range(4):
            out_ref[4 * zh + zl, 0:16, :] = quarters[zl % 2]
            out_ref[4 * zh + zl, 16:32, :] = quarters[zl % 2 + 2]
            out_ref[4 * zh + zl, 32:48, :] = tile


def lay(flat_ref, pieces):
    lane = lax.broadcasted_iota(jnp.int32, (16, 128), 1)
    line = lax.broadcasted_iota(jnp.int32, (16, 128), 0)
    for q in range(4):
        row, off = divmod(2016 * q, 128)
        piece = pieces[q]
        if off:
            piece = pltpu.roll(piece, off, axis=1)
            above = pltpu.roll(piece, 1, axis=0)
            old = flat_ref[row : row + 16, :]
            flat_ref[row + 16 : row + 17, :] = piece[15:16, :]
            piece = jnp.where(lane >= off, piece, jnp.where(line == 0, old, above))
        flat_ref[row : row + 16, :] = piece


def cut(flat_ref, q):
    lane = lax.broadcasted_iota(jnp.int32, (16, 128), 1)
    row, off = divmod(2016 * q, 128)
    here = flat_ref[row : row + 16, :]
    if off:
        after = flat_ref[row + 1 : row + 17, :]
        here = jnp.where(
            lane < 128 - off, pltpu.roll(here, 128 - off, axis=1), pltpu.roll(after, 128 - off, axis=1)
        )
    return here


def step_kernel(
    zb_ref, zh_ref, column_ref, own_ref, other_ref, current_ref, update_ref, out_ref, moment_ref
):
    zb, zh = zb_ref[0], zh_ref[0]
    moment_ref[zb] = own_ref[...]
    moment_ref[1 - zb] = other_ref[...]
    for b in range(2):
        gradient = column_ref[0, 16 * b : 16 * b + 16, :].astype(F32)
        for i in range(1, 16):
            gradient = gradient + column_ref[i, 16 * b : 16 * b + 16, :].astype(F32)
        gradient = gradient * (1.0 / 393216)
        current = current_ref[b]
        first = 0.9 * moment_ref[b, 0] + 0.1 * gradient
        second = 0.95 * moment_ref[b, 1] + 0.05 * gradient * gradient
        update = first / (1.0 - 0.9**STEP) / (jnp.sqrt(second / (1.0 - 0.95**STEP)) + 1e-08)
        stepped = (current - 0.005 * (update + 0.1 * current)).astype(BF16)
        moment_ref[b, 0] = update
        for i in range(16):
            out_ref[i, 16 * b : 16 * b + 16, :] = stepped
    update_ref[...] = moment_ref[zb, 0]
    for slot in range(12):
        tile = column_ref[4 * (zh ^ (slot // 4 + 1)) + slot % 4, 32:48, :]
        for i in range(16):
            out_ref[i, 32 + 16 * slot : 48 + 16 * slot, :] = tile


def stepped_kernel(spread_ref, out_ref):
    out_ref[...] = spread_ref[:, 0:32, :]


def rows_kernel(za_ref, own_ref, other_ref, out_ref, pair_ref, flat_ref, rows_ref):
    za = za_ref[0]
    pair_ref[za] = own_ref[...]
    pair_ref[1 - za] = other_ref[...]
    for p in range(16):
        lay(
            flat_ref.at[p],
            [pair_ref[q % 2, p, 16 * (q // 2) : 16 * (q // 2) + 16, :].astype(F32) for q in range(4)],
        )
        for k in range(9):
            rows_ref[7 * p : 7 * p + 7, 128 * k : 128 * k + 128] = flat_ref[p, pl.ds(k, 7, stride=9), :]
    out_ref[...] = rows_ref[...].astype(BF16)


def input_kernel(core_ref, zh_ref, c_ref, mine_ref, yours_ref, own_ref, other_ref, out_ref, whole_ref, part_ref, sem):
    core, zh = core_ref[0], zh_ref[0]
    for rows_ref, ref, half in ((mine_ref, own_ref, core), (yours_ref, other_ref, 1 - core)):
        whole_ref[pl.ds(pl.multiple_of(224 * zh + 112 * half, 16), 112), :] = rows_ref[...]
        for d in (1, 2, 3):
            for t in range(63):
                low = pl.multiple_of(224 * (zh ^ d) + 112 * half + 16 * (t // 9), 16)
                slot = 32 + 16 * (4 * (d - 1) + t % 4)
                whole_ref[pl.ds(low, 16), 128 * (t % 9) : 128 * (t % 9) + 128] = ref[
                    t // 4, slot : slot + 16, :
                ]
    copies = []
    for i in range(3):
        part_ref[i] = lax.dot_general(
            c_ref[256 * i : 256 * i + 256, :],
            whole_ref[...],
            (((1,), (1,)), ((), ())),
            preferred_element_type=F32,
        ).astype(BF16)
        copies.append(pltpu.make_async_copy(part_ref.at[i], out_ref.at[pl.ds(256 * i, 256)], sem.at[i]))
        copies[-1].start()
    for copy in copies:
        copy.wait()


def call(kernel, outs, operands, specs, scratch=(), out_spec=VMEM):
    return pl.pallas_call(
        kernel,
        out_shape=outs,
        in_specs=specs,
        out_specs=jax.tree.map(lambda _: out_spec, outs),
        scratch_shapes=list(scratch),
        compiler_params=PARAMS,
    )(*operands)


def shards(inputs, cotangent, weight, moment_one, moment_two):
    shape = jax.ShapeDtypeStruct
    core = lax.axis_index("core").astype(jnp.int32).reshape(1)
    za, zb, zh = (lax.axis_index(a).astype(jnp.int32).reshape(1) for a in ("za", "zb", "zh"))
    own = lax.axis_index(("y", "x", "zb", "za"))

    turned = call(turn_kernel, shape((2, 2, 256, 768), BF16), (inputs,), [VMEM])

    def term(half):
        return call(term_kernel, shape((16, 32, 1152), BF16), (half, turned, cotangent), [SMEM, VMEM, VMEM])

    send = term(1 - core)
    got = lax.ppermute(send, "core", [(0, 1), (1, 0)])
    kept = term(core)
    chip = call(add_kernel, shape((16, 32, 1152), BF16), (kept, got), [VMEM, VMEM])
    own_tile = jnp.minimum(own, 62)
    tile = lax.dynamic_slice(weight, (16 * (own_tile // 9), 128 * (own_tile % 9)), (16, 128))
    flat = weight.reshape(-1)
    pair = own // 4 * 4 + lax.axis_index("za")
    current = [lax.dynamic_slice_in_dim(flat, (pair + 2 * b) * 2016, 2016, 0).astype(F32) for b in range(2)]
    current = jnp.stack([jnp.pad(a, (0, 32)).reshape(16, 128) for a in current])
    moments = jnp.stack([jnp.pad(a, (0, 32)).reshape(16, 128) for a in (moment_one, moment_two)])
    moments, mine, chip = lax.optimization_barrier((moments, weight, chip))
    plane = lax.all_to_all(chip, ("y", "x"), 0, 0)
    near = lax.ppermute(moments, "zb", [(0, 1), (1, 0)])
    yours = lax.ppermute(mine, "core", [(0, 1), (1, 0)])
    plane, yours, near = lax.optimization_barrier((plane, yours, near))
    column = call(
        column_kernel,
        shape((16, 48, 128), BF16),
        (plane, tile),
        [VMEM, VMEM],
        [pltpu.VMEM((4, 72, 128), F32)],
    )
    column = lax.all_to_all(column, ("zh", "zb", "za"), 0, 0)
    update, spread = call(
        step_kernel,
        (shape((16, 128), F32), shape((16, 224, 128), BF16)),
        (zb, zh, column, moments, near, current),
        [SMEM] * 2 + [VMEM] * 4,
        [pltpu.VMEM((2, 2, 16, 128), F32)],
    )
    spread = lax.all_to_all(spread, ("y", "x"), 0, 0)
    others = lax.ppermute(spread, "core", [(0, 1), (1, 0)])
    half = call(stepped_kernel, shape((16, 32, 128), BF16), (spread,), [VMEM])
    other = lax.ppermute(half, "za", [(0, 1), (1, 0)])
    grad_in = call(
        input_kernel,
        shape((768, 896), BF16),
        (core, zh, cotangent, weight, yours, spread, others),
        [SMEM] * 2 + [VMEM] * 5,
        [
            pltpu.VMEM((896, 1152), BF16),
            pltpu.VMEM((3, 256, 896), BF16),
            pltpu.SemaphoreType.DMA((3,)),
        ],
        pl.BlockSpec(memory_space=pl.ANY),
    )
    half, other, grad_in = lax.optimization_barrier((half, other, grad_in))
    new_weight = call(
        rows_kernel,
        shape((112, 1152), BF16),
        (za, half, other),
        [SMEM, VMEM, VMEM],
        [pltpu.VMEM((2, 16, 32, 128), BF16), pltpu.VMEM((16, 72, 128), F32), pltpu.VMEM((112, 1152), F32)],
    )
    return (grad_in, update.reshape(2048)[:2016], new_weight)


def solution(mesh):
    fine = Mesh(mesh.devices.reshape(SIZES), AXES)
    return jax.shard_map(
        shards,
        mesh=fine,
        in_specs=(
            P(AXES, None),
            P(AXES, None),
            P(("zh", "core"), None),
            P(AXES),
            P(AXES),
        ),
        out_specs=(P(AXES, None), P(AXES), P(("zh", "core"), None)),
        check_vma=False,
    )
```

```python
import jax
import jax.numpy as jnp
import numpy as np
from jax import lax
from jax.experimental import pallas as pl
from jax.experimental.pallas import tpu as pltpu
from jax.sharding import Mesh, PartitionSpec as P

STEP = 10
AXES = ("zh", "core", "y", "x", "zb", "za")
SIZES = (4, 2, 4, 4, 2, 2)
PLANE, COLUMN = 10, 2
BF16, F32 = jnp.bfloat16, jnp.float32
VMEM = pl.BlockSpec(memory_space=pltpu.VMEM)
SMEM = pl.BlockSpec(memory_space=pltpu.SMEM)
PARAMS = pltpu.CompilerParams(vmem_limit_bytes=16 * 1024 * 1024)


def turn_kernel(x_ref, out_ref):
    for half in range(2):
        for pair in range(2):
            low = 384 * pair
            place = lax.broadcasted_iota(jnp.int32, (256, 512), 0)
            column = lax.broadcasted_iota(jnp.int32, (256, 512), 1)
            row = place & 7
            source = (2 * pair + ((place >> 3) & 1)) * 224 + half * 112 + ((place >> 4) ^ PLANE) * 7 + row - low
            pick = jnp.where((source == column) & (row < 7), 1.0, 0.0).astype(BF16)
            out_ref[half, pair] = lax.dot_general(
                pick, x_ref[:, low : low + 512], (((1,), (1,)), ((), ())), preferred_element_type=F32
            ).astype(BF16)


def term_kernel(half_ref, turned_ref, c_ref, out_ref):
    for pair in range(2):
        part = jnp.dot(turned_ref[half_ref[0], pair], c_ref[...], preferred_element_type=F32).astype(BF16)
        out_ref[:, 16 * pair : 16 * pair + 16, :] = part.reshape(16, 16, 1152)


def add_kernel(kept_ref, got_ref, out_ref):
    for p in range(16):
        out_ref[p] = kept_ref[p] + got_ref[p]


def column_kernel(plane_ref, tile_ref, out_ref, flat_ref):
    total = plane_ref[0].astype(F32)
    for i in range(1, 16):
        total = total + plane_ref[i].astype(F32)
    tile = tile_ref[...]
    for zh in range(4):
        for k in range(9):
            flat_ref[zh, pl.ds(k, 8, stride=9), :] = total[8 * zh : 8 * zh + 8, 128 * k : 128 * k + 128]
        quarters = [cut(flat_ref.at[zh], q).astype(BF16) for q in range(4)]
        for zl in range(4):
            out_ref[4 * (zh ^ COLUMN) + zl, 0:16, :] = quarters[zl % 2]
            out_ref[4 * (zh ^ COLUMN) + zl, 16:32, :] = quarters[zl % 2 + 2]
            out_ref[4 * (zh ^ COLUMN) + zl, 32:48, :] = tile


def lay(flat_ref, pieces):
    lane = lax.broadcasted_iota(jnp.int32, (16, 128), 1)
    line = lax.broadcasted_iota(jnp.int32, (16, 128), 0)
    for q in range(4):
        row, off = divmod(2016 * q, 128)
        piece = pieces[q]
        if off:
            piece = pltpu.roll(piece, off, axis=1)
            above = pltpu.roll(piece, 1, axis=0)
            old = flat_ref[row : row + 16, :]
            flat_ref[row + 16 : row + 17, :] = piece[15:16, :]
            piece = jnp.where(lane >= off, piece, jnp.where(line == 0, old, above))
        flat_ref[row : row + 16, :] = piece


def cut(flat_ref, q):
    lane = lax.broadcasted_iota(jnp.int32, (16, 128), 1)
    row, off = divmod(2016 * q, 128)
    here = flat_ref[row : row + 16, :]
    if off:
        after = flat_ref[row + 1 : row + 17, :]
        here = jnp.where(
            lane < 128 - off, pltpu.roll(here, 128 - off, axis=1), pltpu.roll(after, 128 - off, axis=1)
        )
    return here


def step_kernel(
    zb_ref, zh_ref, column_ref, own_ref, other_ref, current_ref, update_ref, out_ref, moment_ref
):
    zb, zh = zb_ref[0], zh_ref[0]
    moment_ref[zb] = own_ref[...]
    moment_ref[1 - zb] = other_ref[...]
    for b in range(2):
        gradient = column_ref[0, 16 * b : 16 * b + 16, :].astype(F32)
        for i in range(1, 16):
            gradient = gradient + column_ref[i, 16 * b : 16 * b + 16, :].astype(F32)
        gradient = gradient * (1.0 / 393216)
        current = current_ref[b]
        first = 0.9 * moment_ref[b, 0] + 0.1 * gradient
        second = 0.95 * moment_ref[b, 1] + 0.05 * gradient * gradient
        update = first / (1.0 - 0.9**STEP) / (jnp.sqrt(second / (1.0 - 0.95**STEP)) + 1e-08)
        stepped = (current - 0.005 * (update + 0.1 * current)).astype(BF16)
        moment_ref[b, 0] = update
        for i in range(16):
            out_ref[i, 16 * b : 16 * b + 16, :] = stepped
    update_ref[...] = moment_ref[zb, 0]
    for slot in range(12):
        tile = column_ref[4 * (zh ^ (slot // 4 + 1) ^ COLUMN) + slot % 4, 32:48, :]
        for i in range(16):
            out_ref[i, 32 + 16 * slot : 48 + 16 * slot, :] = tile


def stepped_kernel(spread_ref, out_ref):
    out_ref[...] = spread_ref[:, 0:32, :]


def rows_kernel(za_ref, own_ref, other_ref, out_ref, pair_ref, flat_ref, rows_ref):
    za = za_ref[0]
    pair_ref[za] = own_ref[...]
    pair_ref[1 - za] = other_ref[...]
    for p in range(16):
        lay(
            flat_ref.at[p],
            [pair_ref[q % 2, p, 16 * (q // 2) : 16 * (q // 2) + 16, :].astype(F32) for q in range(4)],
        )
        for k in range(9):
            rows_ref[7 * (p ^ PLANE) : 7 * (p ^ PLANE) + 7, 128 * k : 128 * k + 128] = flat_ref[p, pl.ds(k, 7, stride=9), :]
    out_ref[...] = rows_ref[...].astype(BF16)


def input_kernel(core_ref, zh_ref, c_ref, mine_ref, yours_ref, own_ref, other_ref, out_ref, whole_ref, part_ref, sem):
    core, zh = core_ref[0], zh_ref[0]
    for rows_ref, ref, half in ((mine_ref, own_ref, core), (yours_ref, other_ref, 1 - core)):
        whole_ref[pl.ds(pl.multiple_of(224 * zh + 112 * half, 16), 112), :] = rows_ref[...]
        for d in (1, 2, 3):
            for t in range(63):
                low = pl.multiple_of(224 * (zh ^ d) + 112 * half + 16 * (t // 9), 16)
                slot = 32 + 16 * (4 * (d - 1) + t % 4)
                whole_ref[pl.ds(low, 16), 128 * (t % 9) : 128 * (t % 9) + 128] = ref[
                    (t // 4) ^ PLANE, slot : slot + 16, :
                ]
    copies = []
    for i in range(3):
        part_ref[i] = lax.dot_general(
            c_ref[256 * i : 256 * i + 256, :],
            whole_ref[...],
            (((1,), (1,)), ((), ())),
            preferred_element_type=F32,
        ).astype(BF16)
        copies.append(pltpu.make_async_copy(part_ref.at[i], out_ref.at[pl.ds(256 * i, 256)], sem.at[i]))
        copies[-1].start()
    for copy in copies:
        copy.wait()


def call(kernel, outs, operands, specs, scratch=(), out_spec=VMEM):
    return pl.pallas_call(
        kernel,
        out_shape=outs,
        in_specs=specs,
        out_specs=jax.tree.map(lambda _: out_spec, outs),
        scratch_shapes=list(scratch),
        compiler_params=PARAMS,
    )(*operands)


def exchange(a, over):
    ids = np.arange(512).reshape(4, 2, 16, 4)
    if over == "plane":
        groups = ids[:, :, np.arange(16) ^ PLANE].transpose(0, 1, 3, 2).reshape(32, 16)
    else:
        groups = ids[np.arange(4) ^ COLUMN].transpose(1, 2, 0, 3).reshape(32, 16)
    return lax.all_to_all(a, AXES, 0, 0, axis_index_groups=groups.tolist())


def shards(inputs, cotangent, weight, moment_one, moment_two):
    shape = jax.ShapeDtypeStruct
    core = lax.axis_index("core").astype(jnp.int32).reshape(1)
    za, zb, zh = (lax.axis_index(a).astype(jnp.int32).reshape(1) for a in ("za", "zb", "zh"))
    own = lax.axis_index(("y", "x", "zb", "za"))

    turned = call(turn_kernel, shape((2, 2, 256, 768), BF16), (inputs,), [VMEM])

    def term(half):
        return call(term_kernel, shape((16, 32, 1152), BF16), (half, turned, cotangent), [SMEM, VMEM, VMEM])

    send = term(1 - core)
    got = lax.ppermute(send, "core", [(0, 1), (1, 0)])
    kept = term(core)
    chip = call(add_kernel, shape((16, 32, 1152), BF16), (kept, got), [VMEM, VMEM])
    own_tile = jnp.minimum(own, 62)
    tile = lax.dynamic_slice(weight, (16 * (own_tile // 9), 128 * (own_tile % 9)), (16, 128))
    flat = weight.reshape(-1)
    pair = own // 4 * 4 + lax.axis_index("za")
    current = [lax.dynamic_slice_in_dim(flat, (pair + 2 * b) * 2016, 2016, 0).astype(F32) for b in range(2)]
    current = jnp.stack([jnp.pad(a, (0, 32)).reshape(16, 128) for a in current])
    moments = jnp.stack([jnp.pad(a, (0, 32)).reshape(16, 128) for a in (moment_one, moment_two)])
    moments, mine, chip = lax.optimization_barrier((moments, weight, chip))
    plane = exchange(chip, "plane")
    near = lax.ppermute(moments, "zb", [(0, 1), (1, 0)])
    yours = lax.ppermute(mine, "core", [(0, 1), (1, 0)])
    plane, yours, near = lax.optimization_barrier((plane, yours, near))
    column = call(
        column_kernel,
        shape((16, 48, 128), BF16),
        (plane, tile),
        [VMEM, VMEM],
        [pltpu.VMEM((4, 72, 128), F32)],
    )
    column = exchange(column, "column")
    update, spread = call(
        step_kernel,
        (shape((16, 128), F32), shape((16, 224, 128), BF16)),
        (zb, zh, column, moments, near, current),
        [SMEM] * 2 + [VMEM] * 4,
        [pltpu.VMEM((2, 2, 16, 128), F32)],
    )
    spread = exchange(spread, "plane")
    others = lax.ppermute(spread, "core", [(0, 1), (1, 0)])
    half = call(stepped_kernel, shape((16, 32, 128), BF16), (spread,), [VMEM])
    other = lax.ppermute(half, "za", [(0, 1), (1, 0)])
    grad_in = call(
        input_kernel,
        shape((768, 896), BF16),
        (core, zh, cotangent, weight, yours, spread, others),
        [SMEM] * 2 + [VMEM] * 5,
        [
            pltpu.VMEM((896, 1152), BF16),
            pltpu.VMEM((3, 256, 896), BF16),
            pltpu.SemaphoreType.DMA((3,)),
        ],
        pl.BlockSpec(memory_space=pl.ANY),
    )
    half, other, grad_in = lax.optimization_barrier((half, other, grad_in))
    new_weight = call(
        rows_kernel,
        shape((112, 1152), BF16),
        (za, half, other),
        [SMEM, VMEM, VMEM],
        [pltpu.VMEM((2, 16, 32, 128), BF16), pltpu.VMEM((16, 72, 128), F32), pltpu.VMEM((112, 1152), F32)],
    )
    return (grad_in, update.reshape(2048)[:2016], new_weight)


def solution(mesh):
    fine = Mesh(mesh.devices.reshape(SIZES), AXES)
    return jax.shard_map(
        shards,
        mesh=fine,
        in_specs=(
            P(AXES, None),
            P(AXES, None),
            P(("zh", "core"), None),
            P(AXES),
            P(AXES),
        ),
        out_specs=(P(AXES, None), P(AXES), P(("zh", "core"), None)),
        check_vma=False,
    )
```

```python
import jax
import jax.numpy as jnp
import numpy as np
from jax import lax
from jax.experimental import pallas as pl
from jax.experimental.pallas import tpu as pltpu
from jax.sharding import Mesh, PartitionSpec as P

STEP = 10
AXES = ("zh", "core", "y", "x", "zb", "za")
SIZES = (4, 2, 4, 4, 2, 2)
PLANE, SPREAD, COLUMN = 10, 10, 10
BF16, F32 = jnp.bfloat16, jnp.float32
VMEM = pl.BlockSpec(memory_space=pltpu.VMEM)
SMEM = pl.BlockSpec(memory_space=pltpu.SMEM)
PARAMS = pltpu.CompilerParams(vmem_limit_bytes=16 * 1024 * 1024)


def turn_kernel(x_ref, out_ref):
    for half in range(2):
        for pair in range(2):
            low = 384 * pair
            place = lax.broadcasted_iota(jnp.int32, (256, 512), 0)
            column = lax.broadcasted_iota(jnp.int32, (256, 512), 1)
            row = place & 7
            source = (2 * pair + ((place >> 3) & 1)) * 224 + half * 112 + ((place >> 4) ^ PLANE) * 7 + row - low
            pick = jnp.where((source == column) & (row < 7), 1.0, 0.0).astype(BF16)
            out_ref[half, pair] = lax.dot_general(
                pick, x_ref[:, low : low + 512], (((1,), (1,)), ((), ())), preferred_element_type=F32
            ).astype(BF16)


def term_kernel(half_ref, turned_ref, c_ref, out_ref):
    for pair in range(2):
        part = jnp.dot(turned_ref[half_ref[0], pair], c_ref[...], preferred_element_type=F32).astype(BF16)
        out_ref[:, 16 * pair : 16 * pair + 16, :] = part.reshape(16, 16, 1152)


def add_kernel(kept_ref, got_ref, out_ref):
    for p in range(16):
        out_ref[p] = kept_ref[p] + got_ref[p]


def column_kernel(plane_ref, tile_ref, out_ref, flat_ref):
    total = plane_ref[0].astype(F32)
    for i in range(1, 16):
        total = total + plane_ref[i].astype(F32)
    tile = tile_ref[...]
    for zh in range(4):
        for k in range(9):
            flat_ref[zh, pl.ds(k, 8, stride=9), :] = total[8 * zh : 8 * zh + 8, 128 * k : 128 * k + 128]
        quarters = [cut(flat_ref.at[zh], q).astype(BF16) for q in range(4)]
        for zl in range(4):
            out_ref[(4 * zh + zl) ^ COLUMN, 0:16, :] = quarters[zl % 2]
            out_ref[(4 * zh + zl) ^ COLUMN, 16:32, :] = quarters[zl % 2 + 2]
            out_ref[(4 * zh + zl) ^ COLUMN, 32:48, :] = tile


def lay(flat_ref, pieces):
    lane = lax.broadcasted_iota(jnp.int32, (16, 128), 1)
    line = lax.broadcasted_iota(jnp.int32, (16, 128), 0)
    for q in range(4):
        row, off = divmod(2016 * q, 128)
        piece = pieces[q]
        if off:
            piece = pltpu.roll(piece, off, axis=1)
            above = pltpu.roll(piece, 1, axis=0)
            old = flat_ref[row : row + 16, :]
            flat_ref[row + 16 : row + 17, :] = piece[15:16, :]
            piece = jnp.where(lane >= off, piece, jnp.where(line == 0, old, above))
        flat_ref[row : row + 16, :] = piece


def cut(flat_ref, q):
    lane = lax.broadcasted_iota(jnp.int32, (16, 128), 1)
    row, off = divmod(2016 * q, 128)
    here = flat_ref[row : row + 16, :]
    if off:
        after = flat_ref[row + 1 : row + 17, :]
        here = jnp.where(
            lane < 128 - off, pltpu.roll(here, 128 - off, axis=1), pltpu.roll(after, 128 - off, axis=1)
        )
    return here


def step_kernel(
    zb_ref, zh_ref, column_ref, own_ref, other_ref, current_ref, update_ref, out_ref, moment_ref
):
    zb, zh = zb_ref[0], zh_ref[0]
    moment_ref[zb] = own_ref[...]
    moment_ref[1 - zb] = other_ref[...]
    for b in range(2):
        gradient = column_ref[0, 16 * b : 16 * b + 16, :].astype(F32)
        for i in range(1, 16):
            gradient = gradient + column_ref[i, 16 * b : 16 * b + 16, :].astype(F32)
        gradient = gradient * (1.0 / 393216)
        current = current_ref[b]
        first = 0.9 * moment_ref[b, 0] + 0.1 * gradient
        second = 0.95 * moment_ref[b, 1] + 0.05 * gradient * gradient
        update = first / (1.0 - 0.9**STEP) / (jnp.sqrt(second / (1.0 - 0.95**STEP)) + 1e-08)
        stepped = (current - 0.005 * (update + 0.1 * current)).astype(BF16)
        moment_ref[b, 0] = update
        for i in range(16):
            out_ref[i, 16 * b : 16 * b + 16, :] = stepped
    update_ref[...] = moment_ref[zb, 0]
    for slot in range(12):
        tile = column_ref[(4 * (zh ^ (slot // 4 + 1)) + slot % 4) ^ COLUMN, 32:48, :]
        for i in range(16):
            out_ref[i, 32 + 16 * slot : 48 + 16 * slot, :] = tile


def stepped_kernel(spread_ref, out_ref):
    out_ref[...] = spread_ref[:, 0:32, :]


def rows_kernel(za_ref, own_ref, other_ref, out_ref, pair_ref, flat_ref, rows_ref):
    za = za_ref[0]
    pair_ref[za] = own_ref[...]
    pair_ref[1 - za] = other_ref[...]
    for p in range(16):
        lay(
            flat_ref.at[p],
            [pair_ref[q % 2, p, 16 * (q // 2) : 16 * (q // 2) + 16, :].astype(F32) for q in range(4)],
        )
        for k in range(9):
            rows_ref[7 * (p ^ SPREAD) : 7 * (p ^ SPREAD) + 7, 128 * k : 128 * k + 128] = flat_ref[p, pl.ds(k, 7, stride=9), :]
    out_ref[...] = rows_ref[...].astype(BF16)


def input_kernel(core_ref, zh_ref, c_ref, mine_ref, yours_ref, own_ref, other_ref, out_ref, whole_ref, part_ref, sem):
    core, zh = core_ref[0], zh_ref[0]
    for rows_ref, ref, half in ((mine_ref, own_ref, core), (yours_ref, other_ref, 1 - core)):
        whole_ref[pl.ds(pl.multiple_of(224 * zh + 112 * half, 16), 112), :] = rows_ref[...]
        for d in (1, 2, 3):
            for t in range(63):
                low = pl.multiple_of(224 * (zh ^ d) + 112 * half + 16 * (t // 9), 16)
                slot = 32 + 16 * (4 * (d - 1) + t % 4)
                whole_ref[pl.ds(low, 16), 128 * (t % 9) : 128 * (t % 9) + 128] = ref[
                    (t // 4) ^ SPREAD, slot : slot + 16, :
                ]
    copies = []
    for i in range(3):
        part_ref[i] = lax.dot_general(
            c_ref[256 * i : 256 * i + 256, :],
            whole_ref[...],
            (((1,), (1,)), ((), ())),
            preferred_element_type=F32,
        ).astype(BF16)
        copies.append(pltpu.make_async_copy(part_ref.at[i], out_ref.at[pl.ds(256 * i, 256)], sem.at[i]))
        copies[-1].start()
    for copy in copies:
        copy.wait()


def call(kernel, outs, operands, specs, scratch=(), out_spec=VMEM):
    return pl.pallas_call(
        kernel,
        out_shape=outs,
        in_specs=specs,
        out_specs=jax.tree.map(lambda _: out_spec, outs),
        scratch_shapes=list(scratch),
        compiler_params=PARAMS,
    )(*operands)


def exchange(a, over):
    ids = np.arange(512).reshape(4, 2, 16, 4)
    if over == "column":
        groups = ids.transpose(1, 2, 0, 3).reshape(32, 16)[:, np.arange(16) ^ COLUMN]
    else:
        first = PLANE if over == "plane" else SPREAD
        groups = ids[:, :, np.arange(16) ^ first].transpose(0, 1, 3, 2).reshape(32, 16)
    return lax.all_to_all(a, AXES, 0, 0, axis_index_groups=groups.tolist())


def shards(inputs, cotangent, weight, moment_one, moment_two):
    shape = jax.ShapeDtypeStruct
    core = lax.axis_index("core").astype(jnp.int32).reshape(1)
    za, zb, zh = (lax.axis_index(a).astype(jnp.int32).reshape(1) for a in ("za", "zb", "zh"))
    own = lax.axis_index(("y", "x", "zb", "za"))

    turned = call(turn_kernel, shape((2, 2, 256, 768), BF16), (inputs,), [VMEM])

    def term(half):
        return call(term_kernel, shape((16, 32, 1152), BF16), (half, turned, cotangent), [SMEM, VMEM, VMEM])

    send = term(1 - core)
    got = lax.ppermute(send, "core", [(0, 1), (1, 0)])
    kept = term(core)
    chip = call(add_kernel, shape((16, 32, 1152), BF16), (kept, got), [VMEM, VMEM])
    own_tile = jnp.minimum(own, 62)
    tile = lax.dynamic_slice(weight, (16 * (own_tile // 9), 128 * (own_tile % 9)), (16, 128))
    flat = weight.reshape(-1)
    pair = own // 4 * 4 + lax.axis_index("za")
    current = [lax.dynamic_slice_in_dim(flat, (pair + 2 * b) * 2016, 2016, 0).astype(F32) for b in range(2)]
    current = jnp.stack([jnp.pad(a, (0, 32)).reshape(16, 128) for a in current])
    moments = jnp.stack([jnp.pad(a, (0, 32)).reshape(16, 128) for a in (moment_one, moment_two)])
    moments, mine, chip = lax.optimization_barrier((moments, weight, chip))
    plane = exchange(chip, "plane")
    near = lax.ppermute(moments, "zb", [(0, 1), (1, 0)])
    yours = lax.ppermute(mine, "core", [(0, 1), (1, 0)])
    plane, yours, near = lax.optimization_barrier((plane, yours, near))
    column = call(
        column_kernel,
        shape((16, 48, 128), BF16),
        (plane, tile),
        [VMEM, VMEM],
        [pltpu.VMEM((4, 72, 128), F32)],
    )
    column = exchange(column, "column")
    update, spread = call(
        step_kernel,
        (shape((16, 128), F32), shape((16, 224, 128), BF16)),
        (zb, zh, column, moments, near, current),
        [SMEM] * 2 + [VMEM] * 4,
        [pltpu.VMEM((2, 2, 16, 128), F32)],
    )
    spread = exchange(spread, "spread")
    others = lax.ppermute(spread, "core", [(0, 1), (1, 0)])
    half = call(stepped_kernel, shape((16, 32, 128), BF16), (spread,), [VMEM])
    other = lax.ppermute(half, "za", [(0, 1), (1, 0)])
    grad_in = call(
        input_kernel,
        shape((768, 896), BF16),
        (core, zh, cotangent, weight, yours, spread, others),
        [SMEM] * 2 + [VMEM] * 5,
        [
            pltpu.VMEM((896, 1152), BF16),
            pltpu.VMEM((3, 256, 896), BF16),
            pltpu.SemaphoreType.DMA((3,)),
        ],
        pl.BlockSpec(memory_space=pl.ANY),
    )
    half, other, grad_in = lax.optimization_barrier((half, other, grad_in))
    new_weight = call(
        rows_kernel,
        shape((112, 1152), BF16),
        (za, half, other),
        [SMEM, VMEM, VMEM],
        [pltpu.VMEM((2, 16, 32, 128), BF16), pltpu.VMEM((16, 72, 128), F32), pltpu.VMEM((112, 1152), F32)],
    )
    return (grad_in, update.reshape(2048)[:2016], new_weight)


def solution(mesh):
    fine = Mesh(mesh.devices.reshape(SIZES), AXES)
    return jax.shard_map(
        shards,
        mesh=fine,
        in_specs=(
            P(AXES, None),
            P(AXES, None),
            P(("zh", "core"), None),
            P(AXES),
            P(AXES),
        ),
        out_specs=(P(AXES, None), P(AXES), P(("zh", "core"), None)),
        check_vma=False,
    )
```

```python
import jax
import jax.numpy as jnp
import numpy as np
from jax import lax
from jax.experimental import pallas as pl
from jax.experimental.pallas import tpu as pltpu
from jax.sharding import Mesh, PartitionSpec as P

STEP = 10
AXES = ("zh", "core", "y", "x", "zb", "za")
SIZES = (4, 2, 4, 4, 2, 2)
PLANE, SPREAD, COLUMN = 10, 10, 10
BF16, F32 = jnp.bfloat16, jnp.float32
VMEM = pl.BlockSpec(memory_space=pltpu.VMEM)
SMEM = pl.BlockSpec(memory_space=pltpu.SMEM)
PARAMS = pltpu.CompilerParams(vmem_limit_bytes=16 * 1024 * 1024)


def turn_kernel(x_ref, out_ref):
    for half in range(2):
        for pair in range(2):
            low = 384 * pair
            place = lax.broadcasted_iota(jnp.int32, (256, 512), 0)
            column = lax.broadcasted_iota(jnp.int32, (256, 512), 1)
            row = place & 7
            source = (2 * pair + ((place >> 3) & 1)) * 224 + half * 112 + ((place >> 4) ^ PLANE) * 7 + row - low
            pick = jnp.where((source == column) & (row < 7), 1.0, 0.0).astype(BF16)
            out_ref[half, pair] = lax.dot_general(
                pick, x_ref[:, low : low + 512], (((1,), (1,)), ((), ())), preferred_element_type=F32
            ).astype(BF16)


def term_kernel(half_ref, turned_ref, c_ref, out_ref):
    for pair in range(2):
        part = jnp.dot(turned_ref[half_ref[0], pair], c_ref[...], preferred_element_type=F32).astype(BF16)
        out_ref[:, 16 * pair : 16 * pair + 16, :] = part.reshape(16, 16, 1152)


def add_kernel(kept_ref, got_ref, out_ref):
    for p in range(16):
        out_ref[p] = kept_ref[p] + got_ref[p]


def column_kernel(plane_ref, tile_ref, out_ref, flat_ref):
    total = plane_ref[0].astype(F32)
    for i in range(1, 16):
        total = total + plane_ref[i].astype(F32)
    tile = tile_ref[...]
    for zh in range(4):
        for k in range(9):
            flat_ref[zh, pl.ds(k, 8, stride=9), :] = total[8 * zh : 8 * zh + 8, 128 * k : 128 * k + 128]
        quarters = [cut(flat_ref.at[zh], q).astype(BF16) for q in range(4)]
        for zl in range(4):
            out_ref[(4 * zh + zl) ^ COLUMN, 0:16, :] = quarters[zl // 2 * 2]
            out_ref[(4 * zh + zl) ^ COLUMN, 16:32, :] = quarters[zl // 2 * 2 + 1]
            out_ref[(4 * zh + zl) ^ COLUMN, 32:48, :] = tile


def lay(flat_ref, pieces):
    lane = lax.broadcasted_iota(jnp.int32, (16, 128), 1)
    line = lax.broadcasted_iota(jnp.int32, (16, 128), 0)
    for q in range(4):
        row, off = divmod(2016 * q, 128)
        piece = pieces[q]
        if off:
            piece = pltpu.roll(piece, off, axis=1)
            above = pltpu.roll(piece, 1, axis=0)
            old = flat_ref[row : row + 16, :]
            flat_ref[row + 16 : row + 17, :] = piece[15:16, :]
            piece = jnp.where(lane >= off, piece, jnp.where(line == 0, old, above))
        flat_ref[row : row + 16, :] = piece


def cut(flat_ref, q):
    lane = lax.broadcasted_iota(jnp.int32, (16, 128), 1)
    row, off = divmod(2016 * q, 128)
    here = flat_ref[row : row + 16, :]
    if off:
        after = flat_ref[row + 1 : row + 17, :]
        here = jnp.where(
            lane < 128 - off, pltpu.roll(here, 128 - off, axis=1), pltpu.roll(after, 128 - off, axis=1)
        )
    return here


def step_kernel(
    za_ref, zh_ref, column_ref, own_ref, other_ref, current_ref, update_ref, out_ref, moment_ref
):
    za, zh = za_ref[0], zh_ref[0]
    moment_ref[za] = own_ref[...]
    moment_ref[1 - za] = other_ref[...]
    for b in range(2):
        gradient = column_ref[0, 16 * b : 16 * b + 16, :].astype(F32)
        for i in range(1, 16):
            gradient = gradient + column_ref[i, 16 * b : 16 * b + 16, :].astype(F32)
        gradient = gradient * (1.0 / 393216)
        current = current_ref[b]
        first = 0.9 * moment_ref[b, 0] + 0.1 * gradient
        second = 0.95 * moment_ref[b, 1] + 0.05 * gradient * gradient
        update = first / (1.0 - 0.9**STEP) / (jnp.sqrt(second / (1.0 - 0.95**STEP)) + 1e-08)
        stepped = (current - 0.005 * (update + 0.1 * current)).astype(BF16)
        moment_ref[b, 0] = update
        for i in range(16):
            out_ref[i, 16 * b : 16 * b + 16, :] = stepped
    update_ref[...] = moment_ref[za, 0]
    for slot in range(12):
        tile = column_ref[(4 * (zh ^ (slot // 4 + 1)) + slot % 4) ^ COLUMN, 32:48, :]
        for i in range(16):
            out_ref[i, 32 + 16 * slot : 48 + 16 * slot, :] = tile


def stepped_kernel(spread_ref, out_ref):
    out_ref[...] = spread_ref[:, 0:32, :]


def rows_kernel(zb_ref, own_ref, other_ref, out_ref, pair_ref, flat_ref, rows_ref):
    zb = zb_ref[0]
    pair_ref[zb] = own_ref[...]
    pair_ref[1 - zb] = other_ref[...]
    for p in range(16):
        lay(
            flat_ref.at[p],
            [pair_ref[q // 2, p, 16 * (q % 2) : 16 * (q % 2) + 16, :].astype(F32) for q in range(4)],
        )
        for k in range(9):
            rows_ref[7 * (p ^ SPREAD) : 7 * (p ^ SPREAD) + 7, 128 * k : 128 * k + 128] = flat_ref[p, pl.ds(k, 7, stride=9), :]
    out_ref[...] = rows_ref[...].astype(BF16)


def input_kernel(core_ref, zh_ref, c_ref, mine_ref, yours_ref, own_ref, other_ref, out_ref, whole_ref, part_ref, sem):
    core, zh = core_ref[0], zh_ref[0]
    for rows_ref, ref, half in ((mine_ref, own_ref, core), (yours_ref, other_ref, 1 - core)):
        whole_ref[pl.ds(pl.multiple_of(224 * zh + 112 * half, 16), 112), :] = rows_ref[...]
        for d in (1, 2, 3):
            for t in range(63):
                low = pl.multiple_of(224 * (zh ^ d) + 112 * half + 16 * (t // 9), 16)
                slot = 32 + 16 * (4 * (d - 1) + t % 4)
                whole_ref[pl.ds(low, 16), 128 * (t % 9) : 128 * (t % 9) + 128] = ref[
                    (t // 4) ^ SPREAD, slot : slot + 16, :
                ]
    copies = []
    for i in range(3):
        part_ref[i] = lax.dot_general(
            c_ref[256 * i : 256 * i + 256, :],
            whole_ref[...],
            (((1,), (1,)), ((), ())),
            preferred_element_type=F32,
        ).astype(BF16)
        copies.append(pltpu.make_async_copy(part_ref.at[i], out_ref.at[pl.ds(256 * i, 256)], sem.at[i]))
        copies[-1].start()
    for copy in copies:
        copy.wait()


def call(kernel, outs, operands, specs, scratch=(), out_spec=VMEM):
    return pl.pallas_call(
        kernel,
        out_shape=outs,
        in_specs=specs,
        out_specs=jax.tree.map(lambda _: out_spec, outs),
        scratch_shapes=list(scratch),
        compiler_params=PARAMS,
    )(*operands)


def exchange(a, over):
    ids = np.arange(512).reshape(4, 2, 16, 4)
    if over == "column":
        groups = ids.transpose(1, 2, 0, 3).reshape(32, 16)[:, np.arange(16) ^ COLUMN]
    else:
        first = PLANE if over == "plane" else SPREAD
        groups = ids[:, :, np.arange(16) ^ first].transpose(0, 1, 3, 2).reshape(32, 16)
    return lax.all_to_all(a, AXES, 0, 0, axis_index_groups=groups.tolist())


def shards(inputs, cotangent, weight, moment_one, moment_two):
    shape = jax.ShapeDtypeStruct
    core = lax.axis_index("core").astype(jnp.int32).reshape(1)
    za, zb, zh = (lax.axis_index(a).astype(jnp.int32).reshape(1) for a in ("za", "zb", "zh"))
    own = lax.axis_index(("y", "x", "zb", "za"))

    turned = call(turn_kernel, shape((2, 2, 256, 768), BF16), (inputs,), [VMEM])

    def term(half):
        return call(term_kernel, shape((16, 32, 1152), BF16), (half, turned, cotangent), [SMEM, VMEM, VMEM])

    send = term(1 - core)
    got = lax.ppermute(send, "core", [(0, 1), (1, 0)])
    kept = term(core)
    chip = call(add_kernel, shape((16, 32, 1152), BF16), (kept, got), [VMEM, VMEM])
    own_tile = jnp.minimum(own, 62)
    tile = lax.dynamic_slice(weight, (16 * (own_tile // 9), 128 * (own_tile % 9)), (16, 128))
    flat = weight.reshape(-1)
    pair = own // 2 * 2
    current = [lax.dynamic_slice_in_dim(flat, (pair + b) * 2016, 2016, 0).astype(F32) for b in range(2)]
    current = jnp.stack([jnp.pad(a, (0, 32)).reshape(16, 128) for a in current])
    moments = jnp.stack([jnp.pad(a, (0, 32)).reshape(16, 128) for a in (moment_one, moment_two)])
    moments, mine, chip = lax.optimization_barrier((moments, weight, chip))
    plane = exchange(chip, "plane")
    near = lax.ppermute(moments, "za", [(0, 1), (1, 0)])
    yours = lax.ppermute(mine, "core", [(0, 1), (1, 0)])
    plane, yours, near = lax.optimization_barrier((plane, yours, near))
    column = call(
        column_kernel,
        shape((16, 48, 128), BF16),
        (plane, tile),
        [VMEM, VMEM],
        [pltpu.VMEM((4, 72, 128), F32)],
    )
    column = exchange(column, "column")
    update, spread = call(
        step_kernel,
        (shape((16, 128), F32), shape((16, 224, 128), BF16)),
        (za, zh, column, moments, near, current),
        [SMEM] * 2 + [VMEM] * 4,
        [pltpu.VMEM((2, 2, 16, 128), F32)],
    )
    spread = exchange(spread, "spread")
    others = lax.ppermute(spread, "core", [(0, 1), (1, 0)])
    half = call(stepped_kernel, shape((16, 32, 128), BF16), (spread,), [VMEM])
    other = lax.ppermute(half, "zb", [(0, 1), (1, 0)])
    grad_in = call(
        input_kernel,
        shape((768, 896), BF16),
        (core, zh, cotangent, weight, yours, spread, others),
        [SMEM] * 2 + [VMEM] * 5,
        [
            pltpu.VMEM((896, 1152), BF16),
            pltpu.VMEM((3, 256, 896), BF16),
            pltpu.SemaphoreType.DMA((3,)),
        ],
        pl.BlockSpec(memory_space=pl.ANY),
    )
    half, other, grad_in = lax.optimization_barrier((half, other, grad_in))
    new_weight = call(
        rows_kernel,
        shape((112, 1152), BF16),
        (zb, half, other),
        [SMEM, VMEM, VMEM],
        [pltpu.VMEM((2, 16, 32, 128), BF16), pltpu.VMEM((16, 72, 128), F32), pltpu.VMEM((112, 1152), F32)],
    )
    return (grad_in, update.reshape(2048)[:2016], new_weight)


def solution(mesh):
    fine = Mesh(mesh.devices.reshape(SIZES), AXES)
    return jax.shard_map(
        shards,
        mesh=fine,
        in_specs=(
            P(AXES, None),
            P(AXES, None),
            P(("zh", "core"), None),
            P(AXES),
            P(AXES),
        ),
        out_specs=(P(AXES, None), P(AXES), P(("zh", "core"), None)),
        check_vma=False,
    )
```
